256 devices in a mesh: group: 2 (over z_hi), resp: 16 (over y, z_lo), tp: 8 (over x, core).
Axes of the slice: x: 4, y: 4, z: 8 (z_hi: 2, z_lo: 4; z = z_hi * 4 + z_lo), core: 2. Of those that a mesh axis runs over, the one named last changes fastest.
Arguments:
- queries: bfloat16 [4096, 8192], P(('group', 'resp'), 'tp'), parts along dimension 0, may hold values from -8 to 8
- prompt_keys: bfloat16 [8192, 1024], P(('group', 'resp'), 'tp'), parts along dimension 0, may hold values from -8 to 8
- prompt_values: bfloat16 [8192, 1024], P(('group', 'resp'), 'tp'), parts along dimension 0, may hold values from -6 to 6
- resp_keys: bfloat16 [4096, 1024], P(('group', 'resp'), 'tp'), parts along dimension 0, may hold values from -6 to 6
- resp_values: bfloat16 [4096, 1024], P(('group', 'resp'), 'tp'), parts along dimension 0, may hold values from -6 to 6
- grad_out: bfloat16 [4096, 8192], P(('group', 'resp'), 'tp'), parts along dimension 0, may hold values from -24 to 24
- lengths: int32 [32], P(('group', 'resp')), parts along dimension 0, may hold values from 32 to 128, as said below
Outputs:
- grad_queries: bfloat16 [4096, 8192], P(('group', 'resp'), 'tp'), parts along dimension 0
- grad_prompt_keys: bfloat16 [8192, 1024], P(('group', 'resp'), 'tp'), parts along dimension 0
- grad_prompt_values: bfloat16 [8192, 1024], P(('group', 'resp'), 'tp'), parts along dimension 0
- grad_resp_keys: bfloat16 [4096, 1024], P(('group', 'resp'), 'tp'), parts along dimension 0
- grad_resp_values: bfloat16 [4096, 1024], P(('group', 'resp'), 'tp'), parts along dimension 0
The draws below stay inside these ranges and needn't reach their ends.
There are 2 independent parts, one for each index of `group`. The reference program is written for one: setup_inputs(seed, part) draws one part's arguments, and reference() takes and returns one part's arrays. A program takes and returns all parts, laid end to end along the dimension named above; each array names one. Nothing has to cross between parts.
Inputs may be any that keep to these rules, and one draw needn't show every extreme that they name: `lengths`: some response has all 128 tokens live.
All inputs are finite; a program needn't handle non-finite values.
Results may differ from the reference program's by a relative error of at most 0.023.
Values may be sent and summed in bfloat16 or wider, within the bound.
No kernel may reach another device: no remote copies, remote signals or barrier semaphores. Data moves between devices by JAX's collectives and lax.ppermute only.
A program may use at most 64 MiB of HBM per device.

```python
import jax
import jax.numpy as jnp
from jax import lax

HEADS = 64
KV_HEADS = 8
HEAD_DIM = 128
RESP_LEN = 128
RESPONSES = 16
PROMPT = 4096


def draw_queries(key, part):
    key = jax.random.fold_in(key, 11)
    shape = (RESPONSES * RESP_LEN, HEADS * HEAD_DIM)
    values = jnp.clip(jax.random.normal(key, shape, jnp.float32), -6.0, 6.0)
    return values.astype(jnp.bfloat16)


def draw_prompt_keys(key, part):
    key = jax.random.fold_in(key, 12)
    scale_key, value_key = jax.random.split(key)
    shape = (PROMPT, KV_HEADS * HEAD_DIM)
    row_scales = jnp.exp(jax.random.uniform(scale_key, (PROMPT, 1), jnp.float32, jnp.log(0.9), jnp.log(1.1)))
    values = jnp.clip(jax.random.normal(value_key, shape, jnp.float32) * row_scales, -8.0, 8.0)
    return values.astype(jnp.bfloat16)


def draw_lengths(key, part):
    key = jax.random.fold_in(key, 13)
    length_key, full_key = jax.random.split(key)
    drawn = jax.random.randint(length_key, (RESPONSES,), max(RESP_LEN // 4, 1), RESP_LEN + 1)
    full_index = jax.random.randint(full_key, (), 0, RESPONSES)
    return jnp.where(jnp.arange(RESPONSES) == full_index, RESP_LEN, drawn).astype(jnp.int32)


def block_scale(rng, dims, cuts, least, largest):
    def one(position, blocks):
        heights = jax.random.uniform(jax.random.fold_in(jax.random.fold_in(rng, 6), position), (blocks,), jnp.float32, least / len(cuts), largest / len(cuts))
        return jnp.repeat(jnp.exp(heights), dims[position] // blocks).reshape((-1,) + (1,) * (len(dims) - position - 1))

    level = one(*cuts[0])
    for cut in cuts[1:]:
        level = level * one(*cut)
    return level


def scatter_about(stream_key, shape, deviation, most, cuts=(), kind=jnp.bfloat16):
    entries = deviation * jax.random.normal(stream_key, shape, jnp.float32)
    if cuts:
        entries = entries * block_scale(stream_key, shape, cuts, -0.22, 0.18)
    return jnp.clip(entries, -most, most).astype(kind)


def setup_inputs(seed: int = 0, part: int = 0) -> dict:
    keys = jax.random.split(jax.random.key(seed), 8)
    part_keys = jax.random.split(jax.random.fold_in(keys[7], part), 8)
    queries = draw_queries(jax.random.fold_in(jax.random.fold_in(keys[7], part), 71), part)
    prompt_keys = draw_prompt_keys(jax.random.fold_in(jax.random.fold_in(keys[7], part), 71), part)
    prompt_values = scatter_about(part_keys[2], (PROMPT, KV_HEADS * HEAD_DIM), 1.0, 6.0, ((0, 16), (1, 8)))
    resp_keys = scatter_about(part_keys[3], (RESPONSES * RESP_LEN, KV_HEADS * HEAD_DIM), 1.0, 6.0, ((0, 16), (1, 8)))
    resp_values = scatter_about(part_keys[4], (RESPONSES * RESP_LEN, KV_HEADS * HEAD_DIM), 1.0, 6.0, ((0, 16), (1, 8)))
    grad_out = scatter_about(part_keys[5], (RESPONSES * RESP_LEN, HEADS * HEAD_DIM), 4.0, 24.0, ((0, 16), (1, 8)))
    lengths = draw_lengths(jax.random.fold_in(jax.random.fold_in(keys[7], part), 71), part)
    return {"queries": queries, "prompt_keys": prompt_keys, "prompt_values": prompt_values, "resp_keys": resp_keys, "resp_values": resp_values, "grad_out": grad_out, "lengths": lengths}


def attend_one(query, prompt_keys, prompt_values, resp_keys, resp_values, cotangent, live_count):
    scaling = HEAD_DIM ** -0.5
    query_wide = query.astype(jnp.float32)
    pkeys_wide = prompt_keys.astype(jnp.float32)
    pvalues_wide = prompt_values.astype(jnp.float32)
    rkeys_wide = resp_keys.astype(jnp.float32)
    rvalues_wide = resp_values.astype(jnp.float32)
    prompt_scores = jnp.einsum('lge,pe->glp', query_wide, pkeys_wide) * scaling
    resp_scores = jnp.einsum('lge,je->glj', query_wide, rkeys_wide) * scaling
    row_index = jnp.arange(RESP_LEN)[:, None]
    col_index = jnp.arange(RESP_LEN)[None, :]
    causal = col_index <= row_index
    resp_scores = jnp.where(causal[None], resp_scores, -jnp.inf)
    highest = jnp.maximum(jnp.max(prompt_scores, -1), jnp.max(resp_scores, -1))
    prompt_exp = jnp.exp(prompt_scores - highest[..., None])
    resp_exp = jnp.exp(resp_scores - highest[..., None])
    totals = jnp.sum(prompt_exp, -1) + jnp.sum(resp_exp, -1)
    prompt_weights = prompt_exp.astype(jnp.bfloat16).astype(jnp.float32)
    resp_weights = resp_exp.astype(jnp.bfloat16).astype(jnp.float32)
    attended = jnp.einsum('glp,pe->gle', prompt_weights, pvalues_wide) + jnp.einsum('glj,je->gle', resp_weights, rvalues_wide)
    attended = (attended / totals[..., None]).astype(jnp.bfloat16)
    live = (jnp.arange(RESP_LEN) < live_count).astype(jnp.bfloat16)
    masked = cotangent * live[:, None, None]
    masked_wide = masked.astype(jnp.float32)
    delta = jnp.einsum('lge,gle->gl', masked_wide, attended.astype(jnp.float32))
    prompt_probs = prompt_exp / totals[..., None]
    resp_probs = resp_exp / totals[..., None]
    prompt_dp = jnp.einsum('lge,pe->glp', masked_wide, pvalues_wide)
    resp_dp = jnp.einsum('lge,je->glj', masked_wide, rvalues_wide)
    prompt_ds = (prompt_probs * (prompt_dp - delta[..., None])).astype(jnp.bfloat16).astype(jnp.float32)
    resp_ds = (resp_probs * (resp_dp - delta[..., None])).astype(jnp.bfloat16).astype(jnp.float32)
    grad_query = scaling * (jnp.einsum('glp,pe->lge', prompt_ds, pkeys_wide) + jnp.einsum('glj,je->lge', resp_ds, rkeys_wide))
    term_keys = scaling * jnp.einsum('glp,lge->pe', prompt_ds, query_wide)
    term_values = jnp.einsum('glp,lge->pe', prompt_probs.astype(jnp.bfloat16).astype(jnp.float32), masked_wide)
    grad_rkeys = scaling * jnp.einsum('glj,lge->je', resp_ds, query_wide)
    grad_rvalues = jnp.einsum('glj,lge->je', resp_probs.astype(jnp.bfloat16).astype(jnp.float32), masked_wide)
    return (grad_query.astype(jnp.bfloat16), term_keys, term_values,
            grad_rkeys.astype(jnp.bfloat16), grad_rvalues.astype(jnp.bfloat16))


def reference(queries, prompt_keys, prompt_values, resp_keys, resp_values, grad_out, lengths):
    group_size = HEADS // KV_HEADS
    query_heads = queries.reshape(RESPONSES, RESP_LEN, KV_HEADS, group_size, HEAD_DIM).transpose(2, 0, 1, 3, 4)
    grad_heads = grad_out.reshape(RESPONSES, RESP_LEN, KV_HEADS, group_size, HEAD_DIM).transpose(2, 0, 1, 3, 4)
    pkey_heads = prompt_keys.reshape(PROMPT, KV_HEADS, HEAD_DIM).transpose(1, 0, 2)
    pvalue_heads = prompt_values.reshape(PROMPT, KV_HEADS, HEAD_DIM).transpose(1, 0, 2)
    rkey_heads = resp_keys.reshape(RESPONSES, RESP_LEN, KV_HEADS, HEAD_DIM).transpose(2, 0, 1, 3)
    rvalue_heads = resp_values.reshape(RESPONSES, RESP_LEN, KV_HEADS, HEAD_DIM).transpose(2, 0, 1, 3)

    def per_head(inputs):
        query_h, pkey_h, pvalue_h, rkey_h, rvalue_h, grad_h = inputs

        def per_response(carry, items):
            keys_total, values_total = carry
            query_r, rkey_r, rvalue_r, grad_r, live_count = items
            grad_query, term_keys, term_values, grad_rkeys, grad_rvalues = attend_one(
                query_r, pkey_h, pvalue_h, rkey_r, rvalue_r, grad_r, live_count)
            rounded_keys = lax.optimization_barrier(term_keys.astype(jnp.bfloat16)).astype(jnp.float32)
            rounded_values = lax.optimization_barrier(term_values.astype(jnp.bfloat16)).astype(jnp.float32)
            return (keys_total + rounded_keys, values_total + rounded_values), (grad_query, grad_rkeys, grad_rvalues)

        zeros = jnp.zeros((PROMPT, HEAD_DIM), jnp.float32)
        (keys_total, values_total), (grad_query, grad_rkeys, grad_rvalues) = lax.scan(
            per_response, (zeros, zeros), (query_h, rkey_h, rvalue_h, grad_h, lengths))
        return (grad_query, keys_total.astype(jnp.bfloat16), values_total.astype(jnp.bfloat16), grad_rkeys, grad_rvalues)

    grad_query, grad_pkeys, grad_pvalues, grad_rkeys, grad_rvalues = lax.map(
        per_head, (query_heads, pkey_heads, pvalue_heads, rkey_heads, rvalue_heads, grad_heads))
    grad_queries = grad_query.transpose(1, 2, 0, 3, 4).reshape(RESPONSES * RESP_LEN, HEADS * HEAD_DIM)
    grad_prompt_keys = grad_pkeys.transpose(1, 0, 2).reshape(PROMPT, KV_HEADS * HEAD_DIM)
    grad_prompt_values = grad_pvalues.transpose(1, 0, 2).reshape(PROMPT, KV_HEADS * HEAD_DIM)
    grad_resp_keys = grad_rkeys.transpose(1, 2, 0, 3).reshape(RESPONSES * RESP_LEN, KV_HEADS * HEAD_DIM)
    grad_resp_values = grad_rvalues.transpose(1, 2, 0, 3).reshape(RESPONSES * RESP_LEN, KV_HEADS * HEAD_DIM)
    return (grad_queries, grad_prompt_keys, grad_prompt_values, grad_resp_keys, grad_resp_values)
```

```python
import functools

import jax
import jax.numpy as jnp
from jax import lax
from jax.experimental import pallas as pl
from jax.experimental.pallas import tpu as pltpu
from jax.sharding import PartitionSpec as P

HEAD_DIM = 128
SIDE = 4
LOG2E = 1.4426950408889634
BF16 = jnp.bfloat16
F32 = jnp.float32


def dot(a, b, ca, cb):
    return lax.dot_general(a, b, (((ca,), (cb,)), ((), ())), preferred_element_type=F32)


def stack_heads(q_ref):
    heads = q_ref.shape[1] // HEAD_DIM
    return jnp.concatenate([q_ref[:, h * HEAD_DIM : (h + 1) * HEAD_DIM] for h in range(heads)], 0)


def prepare_kernel(len_hbm, q_hbm, g_hbm, k_hbm, v_hbm, kr_hbm, vr_hbm,
                   mt_ref, q_ref, kv_ref, kr_ref, vr_ref, g_ref, len_ref, sems):
    piece = k_hbm.shape[0]
    pairs = (
        (len_hbm, len_ref),
        (g_hbm, g_ref),
        (k_hbm, kv_ref.at[pl.ds(0, piece)]),
        (v_hbm, kv_ref.at[pl.ds(piece, piece)]),
        (q_hbm, q_ref),
        (kr_hbm, kr_ref),
        (vr_hbm, vr_ref),
    )
    copies = [pltpu.make_async_copy(a, b, sems.at[n]) for n, (a, b) in enumerate(pairs)]
    for copy in copies:
        copy.start()
    copies[0].wait()
    copies[1].wait()
    rows, cols = g_ref.shape
    alive = lax.broadcasted_iota(jnp.int32, (rows, cols), 0) < len_ref[0]
    masked = jnp.where(alive, g_ref[...].astype(F32), 0.0)
    for h in range(cols // HEAD_DIM):
        part = masked[:, h * HEAD_DIM : (h + 1) * HEAD_DIM]
        mt_ref[:, h * rows : (h + 1) * rows] = part.T.astype(BF16)
    for copy in copies[2:]:
        copy.wait()


def plane_of(pieces, part):
    size = pieces[0].shape[0] // 2
    return jnp.concatenate([p[part * size : (part + 1) * size, :] for p in pieces], 0)


def score_block(s_ref, base, keys, q, highest, mask=None):
    group = highest.shape[0]
    step = min(256, keys.shape[0])
    for r in range(0, keys.shape[0], step):
        s = dot(keys[r : r + step, :], q, 1, 1)
        if mask is not None:
            s = jnp.where(mask, s, -jnp.inf)
        s_ref[base + r : base + r + step, :] = s
        highest = jnp.maximum(highest, jnp.max(s.reshape(step // group, group, s.shape[1]), 0))
    return highest


def weigh(s_ref, w_ref, highest):
    group, step = 16, 64
    scale = HEAD_DIM**-0.5 * LOG2E
    totals = jnp.zeros((group, s_ref.shape[1]), F32)
    for r in range(0, s_ref.shape[0], step):
        w = jnp.exp2((s_ref[r : r + step, :] - highest) * scale)
        w_ref[r : r + step, :] = w.astype(BF16)
        totals = totals + jnp.sum(w.reshape(step // group, group, w.shape[1]), 0)
    return jnp.sum(totals, 0, keepdims=True)


def summary(highest, totals, attended, n, high_ref, lse_ref, a_ref):
    high = highest * (HEAD_DIM**-0.5 * LOG2E)
    high_ref[n : n + 1, :] = high
    lse_ref[n : n + 1, :] = high + jnp.log2(totals)
    a_ref[...] = attended / totals


def own_kernel(q_ref, kr, vr, p0, p1, p2, p3, w_ref, high_ref, lse_ref, a_ref, s_ref):
    rows = kr.shape[0]
    wide = w_ref.shape[1]
    pieces = (p0, p1, p2, p3)
    q = stack_heads(q_ref)
    key_pos = lax.broadcasted_iota(jnp.int32, (rows, wide), 0)
    token = lax.broadcasted_iota(jnp.int32, (rows, wide), 1) % rows
    highest = jnp.full((16, wide), -jnp.inf, F32)
    highest = score_block(s_ref, 0, kr, q, highest, key_pos <= token)
    highest = score_block(s_ref, rows, plane_of(pieces, 0), q, highest)
    highest = jnp.max(highest, 0, keepdims=True)
    totals = weigh(s_ref, w_ref, highest)
    attended = dot(vr[...], w_ref[0:rows, :], 0, 0) + dot(
        plane_of(pieces, 1), w_ref[rows:, :], 0, 0
    )
    summary(highest, totals, attended, 0, high_ref, lse_ref, a_ref)


def other_kernel(q1, q2, q3, p0, p1, p2, p3, w1, w2, w3, high_ref, lse_ref, a1, a2, a3, s1, s2, s3):
    pieces = (p0, p1, p2, p3)
    keys, values = plane_of(pieces, 0), plane_of(pieces, 1)
    for n, (q, w, a, s_ref) in enumerate(((q1, w1, a1, s1), (q2, w2, a2, s2), (q3, w3, a3, s3))):
        highest = jnp.full((16, w.shape[1]), -jnp.inf, F32)
        highest = score_block(s_ref, 0, keys, stack_heads(q), highest)
        highest = jnp.max(highest, 0, keepdims=True)
        totals = weigh(s_ref, w, highest)
        summary(highest, totals, dot(values, w[...], 0, 0), n, high_ref, lse_ref, a)


def delta_kernel(high0, high123, lse0, lse123, a0, a1, a2, a3, m0, m1, m2, m3, high_ref, stat_ref):
    high_ref[0:1, :] = high0[...]
    high_ref[1:SIDE, :] = high123[...]
    stat_ref[0:1, :] = lse0[...]
    for d, (a, m) in enumerate(zip((a0, a1, a2, a3), (m0, m1, m2, m3))):
        if d:
            stat_ref[2 * d : 2 * d + 1, :] = lse123[d - 1 : d, :]
        part = jnp.sum(m[...].astype(F32) * a[...], 0, keepdims=True)
        stat_ref[2 * d + 1 : 2 * d + 2, :] = part


def product_kernel(stat_ref, p0, p1, p2, p3, vr, m0, m1, m2, m3, x0, x1, x2, x3, xr):
    values = plane_of((p0, p1, p2, p3), 1)
    for m, x in ((m1, x1), (m3, x3), (m2, x2), (m0, x0)):
        x[...] = dot(values, m[...], 1, 0)
    xr[...] = dot(vr[...], m0[...], 1, 0)


def settle(stats, high_ref, d):
    parts = []
    for e, ref in enumerate(stats):
        row = 2 * ((d - e) % SIDE)
        parts.append((ref[row : row + 1, :], ref[row + 1 : row + 2, :]))
    highest = parts[0][0]
    for lse, term in parts[1:]:
        highest = jnp.maximum(highest, lse)
    totals = jnp.zeros_like(highest)
    delta = jnp.zeros_like(highest)
    for lse, term in parts:
        share = jnp.exp2(lse - highest)
        totals = totals + share
        delta = delta + term * share
    return jnp.exp2(high_ref[d : d + 1, :] - highest) / totals, delta / totals


def turn_back(total, out):
    rows = out.shape[0]
    total = total * HEAD_DIM**-0.5
    for h in range(total.shape[1] // rows):
        part = total[:, h * rows : (h + 1) * rows]
        out[:, h * HEAD_DIM : (h + 1) * HEAD_DIM] = part.T.astype(BF16)


def remote_kernel(t0, t1, t2, t3, high_ref, p0, p1, p2, p3, w2, x2,
                  factor_ref, delta_ref, q2, ds2):
    stats = (t0, t1, t2, t3)
    for d in range(SIDE):
        factor, delta = settle(stats, high_ref, d)
        factor_ref[d : d + 1, :] = factor
        delta_ref[d : d + 1, :] = delta
        if d == 2:
            ds = w2[...] * ((x2[...] - delta) * factor).astype(BF16)
            ds2[...] = ds
            turn_back(dot(plane_of((p0, p1, p2, p3), 0), ds, 0, 0), q2)


def local_kernel(factor_ref, delta_ref, p0, p1, p2, p3, kr, w0, w1, w2, w3, x0, x1, x3, xr, ds2,
                 m0, m1, m2, m3, q0, q1, q2, q3, dq0, dq1, dq3, dkr_ref, dvr_ref, o0, o1, o2, o3):
    rows = kr.shape[0]
    size = p0.shape[0] // 2
    scale = HEAD_DIM**-0.5
    plane_keys = plane_of((p0, p1, p2, p3), 0)

    def pair(d):
        return factor_ref[d : d + 1, :], delta_ref[d : d + 1, :]

    def masked(m, d):
        return (m[...].astype(F32) * factor_ref[d : d + 1, :]).astype(BF16)

    keys = dot(ds2[...], stack_heads(q2), 1, 0)
    values = dot(w2[...], masked(m2, 2), 1, 1)
    for d, q, m, w, x, out in ((1, q1, m1, w1, x1, dq1), (3, q3, m3, w3, x3, dq3)):
        factor, delta = pair(d)
        ds = w[...] * ((x[...] - delta) * factor).astype(BF16)
        turn_back(dot(plane_keys, ds, 0, 0), out)
        keys = keys + dot(ds, stack_heads(q), 1, 0)
        values = values + dot(w[...], masked(m, d), 1, 1)
    factor, delta = pair(0)
    q = stack_heads(q0)
    g = masked(m0, 0)
    near = w0[0:rows, :]
    ds = near * ((xr[...] - delta) * factor).astype(BF16)
    dvr_ref[...] = dot(near, g, 1, 1).astype(BF16)
    dkr_ref[...] = (dot(ds, q, 1, 0) * scale).astype(BF16)
    grad = dot(kr[...], ds, 0, 0)
    ds = w0[rows:, :] * ((x0[...] - delta) * factor).astype(BF16)
    turn_back(grad + dot(plane_keys, ds, 0, 0), dq0)
    keys = ((keys + dot(ds, q, 1, 0)) * scale).astype(BF16)
    values = (values + dot(w0[rows:, :], g, 1, 1)).astype(BF16)
    for d, out in enumerate((o0, o1, o2, o3)):
        out[0:size, :] = keys[d * size : (d + 1) * size, :]
        out[size : 2 * size, :] = values[d * size : (d + 1) * size, :]


def shift_y(d):
    return [(y * SIDE + z, (y + d) % SIDE * SIDE + z) for y in range(SIDE) for z in range(SIDE)]


def shift_z(d):
    return [(y * SIDE + z, y * SIDE + (z + d) % SIDE) for y in range(SIDE) for z in range(SIDE)]


def send(x, perm):
    return lax.ppermute(x, "resp", perm)


def combine(own, received):
    own = own.astype(F32)
    for x in received:
        own = own + x.astype(F32)
    return own.astype(BF16)


def from_others(x, shift):
    one, three, two = (send(x, shift(d)) for d in (1, 3, 2))
    return one, two, three


def call(kernel, name, outs, inputs, memory, scratch=(), flops=0, exps=0, space=pltpu.VMEM):
    return pl.pallas_call(
        kernel,
        out_shape=[jax.ShapeDtypeStruct(*o) for o in outs],
        in_specs=[pl.BlockSpec(memory_space=space)] * len(inputs),
        out_specs=[pl.BlockSpec(memory_space=pltpu.VMEM)] * len(outs),
        scratch_shapes=list(scratch),
        compiler_params=pltpu.CompilerParams(vmem_limit_bytes=memory * 2**20),
        cost_estimate=pl.CostEstimate(flops=flops, bytes_accessed=2**20, transcendentals=exps),
        name=name,
    )(*inputs)


def body(queries, prompt_keys, prompt_values, resp_keys, resp_values, grad_out, lengths):
    rows, cols = queries.shape
    part = prompt_keys.shape[0]
    plane = SIDE * part
    wide = rows * cols // HEAD_DIM
    near = plane + rows
    unit = 2 * wide * plane * HEAD_DIM
    turned = ((HEAD_DIM, wide), BF16)
    turned_wide = ((HEAD_DIM, wide), F32)
    small = ((rows, HEAD_DIM), BF16)
    flat = ((rows, cols), BF16)
    both = ((2 * part, HEAD_DIM), BF16)
    square = ((plane, wide), BF16)
    square_wide = ((plane, wide), F32)
    scores = pltpu.VMEM((plane, wide), F32)

    q1, q3 = (send(queries, shift_y(d)) for d in (1, 3))
    q2 = send(q1, shift_y(1))
    params = (queries, grad_out, prompt_keys, prompt_values, resp_keys, resp_values)
    m0, q0, piece, kr, vr = call(
        prepare_kernel, "prepare", [turned, flat, both, small, small],
        [lengths] + [pltpu.with_memory_space_constraint(x, pltpu.HBM) for x in params], 8,
        [pltpu.VMEM((rows, cols), BF16), pltpu.SMEM((1,), jnp.int32),
         pltpu.SemaphoreType.DMA((7,))], space=pltpu.HBM)
    p1, p3 = (send(piece, shift_z(d)) for d in (1, 3))
    pieces = (piece, p1, send(p1, shift_z(1)), p3)
    m1, m3 = (send(m0, shift_y(d)) for d in (1, 3))
    m2 = send(m3, shift_y(3))
    w0, high0, lse0, a0 = call(
        own_kernel, "own", [((near, wide), BF16), ((1, wide), F32), ((1, wide), F32), turned_wide],
        (q0, kr, vr, *pieces), 16, [pltpu.VMEM((near, wide), F32)],
        flops=2 * unit, exps=near * wide)
    w1, w2, w3, high, lse, a1, a2, a3 = call(
        other_kernel, "other",
        [square] * 3 + [((SIDE - 1, wide), F32)] * 2 + [turned_wide] * 3,
        (q1, q2, q3, *pieces), 28, [scores] * 3, flops=6 * unit, exps=3 * plane * wide)
    high, stat = call(
        delta_kernel, "delta", [((SIDE, wide), F32), ((2 * SIDE, wide), F32)],
        (high0, high, lse0, lse, a0, a1, a2, a3, m0, m1, m2, m3), 8, flops=unit // 2)
    all_stats = (stat, *from_others(stat, shift_y))
    x0, x1, x2, x3, xr = call(
        product_kernel, "product", [square_wide] * 4 + [((rows, wide), F32)],
        (stat, *pieces, vr, m0, m1, m2, m3), 12, flops=4 * unit)
    factors, delta, dq2, ds2 = call(
        remote_kernel, "remote",
        [((SIDE, wide), F32)] * 2 + [flat, square],
        (*all_stats, high, *pieces, w2, x2), 12, flops=unit)
    back2 = send(dq2, shift_y(-2))
    dq0, dq1, dq3, dkr, dvr, o0, o1, o2, o3 = call(
        local_kernel, "local", [flat] * 3 + [small, small] + [both] * 4,
        (factors, delta, *pieces, kr, w0, w1, w2, w3, x0, x1, x3, xr, ds2,
         m0, m1, m2, m3, q0, q1, q2, q3), 16, flops=11 * unit)
    o2, unused = lax.optimization_barrier((o2, back2))
    total = combine(o0, [send(x, shift_z(-d)) for d, x in ((1, o1), (3, o3), (2, o2))])
    returned = [send(x, shift_y(-d)) for d, x in ((1, dq1), (3, dq3))] + [back2]
    grad_queries = combine(dq0, returned)
    return grad_queries, total[:part], total[part:], dkr, dvr


def solution(mesh):
    spec = P(("group", "resp"), "tp")
    return jax.shard_map(
        body,
        mesh=mesh,
        in_specs=(spec,) * 6 + (P(("group", "resp")),),
        out_specs=(spec,) * 5,
        check_vma=False,
    )
```

```python
import functools

import jax
import jax.numpy as jnp
from jax import lax
from jax.experimental import pallas as pl
from jax.experimental.pallas import tpu as pltpu
from jax.sharding import PartitionSpec as P

HEAD_DIM = 128
SIDE = 4
LOG2E = 1.4426950408889634
BF16 = jnp.bfloat16
F32 = jnp.float32


def dot(a, b, ca, cb):
    return lax.dot_general(a, b, (((ca,), (cb,)), ((), ())), preferred_element_type=F32)


def stack_heads(q_ref):
    heads = q_ref.shape[1] // HEAD_DIM
    return jnp.concatenate([q_ref[:, h * HEAD_DIM : (h + 1) * HEAD_DIM] for h in range(heads)], 0)


def prepare_kernel(len_hbm, q_hbm, g_hbm, k_hbm, v_hbm, kr_hbm, vr_hbm,
                   mt_ref, q_ref, kv_ref, kr_ref, vr_ref, g_ref, len_ref, sems):
    piece = k_hbm.shape[0]
    pairs = (
        (len_hbm, len_ref),
        (g_hbm, g_ref),
        (k_hbm, kv_ref.at[pl.ds(0, piece)]),
        (v_hbm, kv_ref.at[pl.ds(piece, piece)]),
        (q_hbm, q_ref),
        (kr_hbm, kr_ref),
        (vr_hbm, vr_ref),
    )
    copies = [pltpu.make_async_copy(a, b, sems.at[n]) for n, (a, b) in enumerate(pairs)]
    for copy in copies:
        copy.start()
    copies[0].wait()
    copies[1].wait()
    rows, cols = g_ref.shape
    alive = lax.broadcasted_iota(jnp.int32, (rows, cols), 0) < len_ref[0]
    masked = jnp.where(alive, g_ref[...].astype(F32), 0.0)
    for h in range(cols // HEAD_DIM):
        part = masked[:, h * HEAD_DIM : (h + 1) * HEAD_DIM]
        mt_ref[:, h * rows : (h + 1) * rows] = part.T.astype(BF16)
    for copy in copies[2:]:
        copy.wait()


def plane_of(pieces, part):
    size = pieces[0].shape[0] // 2
    return jnp.concatenate([p[part * size : (part + 1) * size, :] for p in pieces], 0)


def score_block(s_ref, base, keys, q, highest, mask=None):
    group = highest.shape[0]
    step = min(256, keys.shape[0])
    for r in range(0, keys.shape[0], step):
        s = dot(keys[r : r + step, :], q, 1, 1)
        if mask is not None:
            s = jnp.where(mask, s, -jnp.inf)
        s_ref[base + r : base + r + step, :] = s
        highest = jnp.maximum(highest, jnp.max(s.reshape(step // group, group, s.shape[1]), 0))
    return highest


def weigh(s_ref, w_ref, highest):
    group, step = 16, 64
    scale = HEAD_DIM**-0.5 * LOG2E
    totals = jnp.zeros((group, s_ref.shape[1]), F32)
    for r in range(0, s_ref.shape[0], step):
        w = jnp.exp2((s_ref[r : r + step, :] - highest) * scale)
        w_ref[r : r + step, :] = w.astype(BF16)
        totals = totals + jnp.sum(w.reshape(step // group, group, w.shape[1]), 0)
    return jnp.sum(totals, 0, keepdims=True)


def summary(highest, totals, n, high_ref, lse_ref):
    high = highest * (HEAD_DIM**-0.5 * LOG2E)
    high_ref[n : n + 1, :] = high
    lse_ref[n : n + 1, :] = high + jnp.log2(totals)


def own_kernel(q_ref, kr, vr, p0, p1, p2, p3, w_ref, high_ref, lse_ref, a_ref, s_ref):
    rows = kr.shape[0]
    wide = w_ref.shape[1]
    pieces = (p0, p1, p2, p3)
    q = stack_heads(q_ref)
    key_pos = lax.broadcasted_iota(jnp.int32, (rows, wide), 0)
    token = lax.broadcasted_iota(jnp.int32, (rows, wide), 1) % rows
    highest = jnp.full((16, wide), -jnp.inf, F32)
    highest = score_block(s_ref, 0, kr, q, highest, key_pos <= token)
    highest = score_block(s_ref, rows, plane_of(pieces, 0), q, highest)
    highest = jnp.max(highest, 0, keepdims=True)
    totals = weigh(s_ref, w_ref, highest)
    summary(highest, totals, 0, high_ref, lse_ref)
    a_ref[...] = dot(vr[...], w_ref[0:rows, :], 0, 0) + dot(
        plane_of(pieces, 1), w_ref[rows:, :], 0, 0
    )


def other_kernel(q1, q2, q3, p0, p1, p2, p3, w1, w2, w3, high_ref, lse_ref, a1, a2, a3, s1, s2, s3):
    pieces = (p0, p1, p2, p3)
    keys, values = plane_of(pieces, 0), plane_of(pieces, 1)
    plane, wide = w1.shape
    group, step, small = 16, 256, 64
    scale = HEAD_DIM**-0.5 * LOG2E
    jobs = ((q1, w1, a1, s1), (q2, w2, a2, s2), (q3, w3, a3, s3))
    before = None
    for n in range(len(jobs) + 1):
        if n < len(jobs):
            q = stack_heads(jobs[n][0])
            top = jnp.full((group, wide), -jnp.inf, F32)
        totals = jnp.zeros((group, wide), F32)
        for r in range(0, plane, step):
            if n < len(jobs):
                s = dot(keys[r : r + step, :], q, 1, 1)
                jobs[n][3][r : r + step, :] = s
                top = jnp.maximum(top, jnp.max(s.reshape(step // group, group, wide), 0))
            if before is not None:
                for t in range(r, r + step, small):
                    w = jnp.exp2((jobs[n - 1][3][t : t + small, :] - before) * scale)
                    jobs[n - 1][1][t : t + small, :] = w.astype(BF16)
                    totals = totals + jnp.sum(w.reshape(small // group, group, wide), 0)
        if before is not None:
            summary(before, jnp.sum(totals, 0, keepdims=True), n - 1, high_ref, lse_ref)
            jobs[n - 1][2][...] = dot(values, jobs[n - 1][1][...], 0, 0)
        if n < len(jobs):
            before = jnp.max(top, 0, keepdims=True)


def delta_kernel(high0, high123, lse0, lse123, a0, a1, a2, a3, m0, m1, m2, m3, high_ref, stat_ref):
    high_ref[0:1, :] = high0[...]
    high_ref[1:SIDE, :] = high123[...]
    for d, (a, m) in enumerate(zip((a0, a1, a2, a3), (m0, m1, m2, m3))):
        lse = lse123[d - 1 : d, :] if d else lse0[...]
        stat_ref[2 * d : 2 * d + 1, :] = lse
        part = jnp.sum(m[...].astype(F32) * a[...], 0, keepdims=True)
        part = part * jnp.exp2(high_ref[d : d + 1, :] - lse)
        stat_ref[2 * d + 1 : 2 * d + 2, :] = part


def product_kernel(stat_ref, p0, p1, p2, p3, vr, m0, m1, m2, m3, x0, x1, x2, x3, xr):
    values = plane_of((p0, p1, p2, p3), 1)
    for m, x in ((m1, x1), (m3, x3), (m2, x2), (m0, x0)):
        x[...] = dot(values, m[...], 1, 0)
    xr[...] = dot(vr[...], m0[...], 1, 0)


def settle(stats, high_ref, d):
    parts = []
    for e, ref in enumerate(stats):
        row = 2 * ((d - e) % SIDE)
        parts.append((ref[row : row + 1, :], ref[row + 1 : row + 2, :]))
    highest = parts[0][0]
    for lse, term in parts[1:]:
        highest = jnp.maximum(highest, lse)
    totals = jnp.zeros_like(highest)
    delta = jnp.zeros_like(highest)
    for lse, term in parts:
        share = jnp.exp2(lse - highest)
        totals = totals + share
        delta = delta + term * share
    return jnp.exp2(high_ref[d : d + 1, :] - highest) / totals, delta / totals


def turn_back(total, out):
    rows = out.shape[0]
    total = total * HEAD_DIM**-0.5
    for h in range(total.shape[1] // rows):
        part = total[:, h * rows : (h + 1) * rows]
        out[:, h * HEAD_DIM : (h + 1) * HEAD_DIM] = part.T.astype(BF16)


def remote_kernel(t0, t1, t2, t3, high_ref, p0, p1, p2, p3, w2, x2,
                  factor_ref, delta_ref, q2, ds2):
    stats = (t0, t1, t2, t3)
    for d in range(SIDE):
        factor, delta = settle(stats, high_ref, d)
        factor_ref[d : d + 1, :] = factor
        delta_ref[d : d + 1, :] = delta
        if d == 2:
            ds = w2[...] * ((x2[...] - delta) * factor).astype(BF16)
            ds2[...] = ds
            turn_back(dot(plane_of((p0, p1, p2, p3), 0), ds, 0, 0), q2)


def local_kernel(factor_ref, delta_ref, p0, p1, p2, p3, kr, w0, w1, w2, w3, x0, x1, x3, xr, ds2,
                 m0, m1, m2, m3, q0, q1, q2, q3, dq0, dq1, dq3, dkr_ref, dvr_ref, o0, o1, o2, o3):
    rows = kr.shape[0]
    size = p0.shape[0] // 2
    scale = HEAD_DIM**-0.5
    plane_keys = plane_of((p0, p1, p2, p3), 0)

    def pair(d):
        return factor_ref[d : d + 1, :], delta_ref[d : d + 1, :]

    def masked(m, d):
        return (m[...].astype(F32) * factor_ref[d : d + 1, :]).astype(BF16)

    plane = w1.shape[0]
    step = 512
    starts = range(0, plane, step)
    q, g = stack_heads(q2), masked(m2, 2)
    keys = [dot(ds2[r : r + step, :], q, 1, 0) for r in starts]
    values = [dot(w2[r : r + step, :], g, 1, 1) for r in starts]
    for d, q, m, w, x, out in ((1, q1, m1, w1, x1, dq1), (3, q3, m3, w3, x3, dq3)):
        factor, delta = pair(d)
        q, g = stack_heads(q), masked(m, d)
        grad = None
        for n, r in enumerate(starts):
            rows_r = slice(r, r + step)
            ds = w[rows_r, :] * ((x[rows_r, :] - delta) * factor).astype(BF16)
            values[n] = values[n] + dot(w[rows_r, :], g, 1, 1)
            keys[n] = keys[n] + dot(ds, q, 1, 0)
            part = dot(plane_keys[rows_r, :], ds, 0, 0)
            grad = part if grad is None else grad + part
        turn_back(grad, out)
    keys, values = jnp.concatenate(keys, 0), jnp.concatenate(values, 0)
    factor, delta = pair(0)
    q = stack_heads(q0)
    g = masked(m0, 0)
    near = w0[0:rows, :]
    ds = near * ((xr[...] - delta) * factor).astype(BF16)
    dvr_ref[...] = dot(near, g, 1, 1).astype(BF16)
    dkr_ref[...] = (dot(ds, q, 1, 0) * scale).astype(BF16)
    grad = dot(kr[...], ds, 0, 0)
    ds = w0[rows:, :] * ((x0[...] - delta) * factor).astype(BF16)
    turn_back(grad + dot(plane_keys, ds, 0, 0), dq0)
    keys = ((keys + dot(ds, q, 1, 0)) * scale).astype(BF16)
    values = (values + dot(w0[rows:, :], g, 1, 1)).astype(BF16)
    for d, out in enumerate((o0, o1, o2, o3)):
        out[0:size, :] = keys[d * size : (d + 1) * size, :]
        out[size : 2 * size, :] = values[d * size : (d + 1) * size, :]


def shift_y(d):
    return [(y * SIDE + z, (y + d) % SIDE * SIDE + z) for y in range(SIDE) for z in range(SIDE)]


def shift_z(d):
    return [(y * SIDE + z, y * SIDE + (z + d) % SIDE) for y in range(SIDE) for z in range(SIDE)]


def send(x, perm):
    return lax.ppermute(x, "resp", perm)


def combine(own, received):
    own = own.astype(F32)
    for x in received:
        own = own + x.astype(F32)
    return own.astype(BF16)


def from_others(x, shift):
    one, three, two = (send(x, shift(d)) for d in (1, 3, 2))
    return one, two, three


def call(kernel, name, outs, inputs, memory, scratch=(), flops=0, exps=0, space=pltpu.VMEM):
    return pl.pallas_call(
        kernel,
        out_shape=[jax.ShapeDtypeStruct(*o) for o in outs],
        in_specs=[pl.BlockSpec(memory_space=space)] * len(inputs),
        out_specs=[pl.BlockSpec(memory_space=pltpu.VMEM)] * len(outs),
        scratch_shapes=list(scratch),
        compiler_params=pltpu.CompilerParams(vmem_limit_bytes=memory * 2**20),
        cost_estimate=pl.CostEstimate(flops=flops, bytes_accessed=2**20, transcendentals=exps),
        name=name,
    )(*inputs)


def body(queries, prompt_keys, prompt_values, resp_keys, resp_values, grad_out, lengths):
    rows, cols = queries.shape
    part = prompt_keys.shape[0]
    plane = SIDE * part
    wide = rows * cols // HEAD_DIM
    near = plane + rows
    unit = 2 * wide * plane * HEAD_DIM
    turned = ((HEAD_DIM, wide), BF16)
    turned_wide = ((HEAD_DIM, wide), F32)
    small = ((rows, HEAD_DIM), BF16)
    flat = ((rows, cols), BF16)
    both = ((2 * part, HEAD_DIM), BF16)
    square = ((plane, wide), BF16)
    square_wide = ((plane, wide), F32)
    scores = pltpu.VMEM((plane, wide), F32)

    q1, q3 = (send(queries, shift_y(d)) for d in (1, 3))
    q2 = send(q1, shift_y(1))
    params = (queries, grad_out, prompt_keys, prompt_values, resp_keys, resp_values)
    m0, q0, piece, kr, vr = call(
        prepare_kernel, "prepare", [turned, flat, both, small, small],
        [lengths] + [pltpu.with_memory_space_constraint(x, pltpu.HBM) for x in params], 8,
        [pltpu.VMEM((rows, cols), BF16), pltpu.SMEM((1,), jnp.int32),
         pltpu.SemaphoreType.DMA((7,))], space=pltpu.HBM)
    p1, p3 = (send(piece, shift_z(d)) for d in (1, 3))
    pieces = (piece, p1, send(p3, shift_z(3)), p3)
    m1, m3 = (send(m0, shift_y(d)) for d in (1, 3))
    m2 = send(m3, shift_y(3))
    w0, high0, lse0, a0 = call(
        own_kernel, "own", [((near, wide), BF16), ((1, wide), F32), ((1, wide), F32), turned_wide],
        (q0, kr, vr, *pieces), 16, [pltpu.VMEM((near, wide), F32)],
        flops=2 * unit, exps=near * wide)
    w1, w2, w3, high, lse, a1, a2, a3 = call(
        other_kernel, "other",
        [square] * 3 + [((SIDE - 1, wide), F32)] * 2 + [turned_wide] * 3,
        (q1, q2, q3, *pieces), 28, [scores] * 3, flops=6 * unit, exps=3 * plane * wide)
    high, stat = call(
        delta_kernel, "delta", [((SIDE, wide), F32), ((2 * SIDE, wide), F32)],
        (high0, high, lse0, lse, a0, a1, a2, a3, m0, m1, m2, m3), 8, flops=unit // 2)
    all_stats = (stat, *from_others(stat, shift_y))
    x0, x1, x2, x3, xr = call(
        product_kernel, "product", [square_wide] * 4 + [((rows, wide), F32)],
        (stat, *pieces, vr, m0, m1, m2, m3), 12, flops=4 * unit)
    factors, delta, dq2, ds2 = call(
        remote_kernel, "remote",
        [((SIDE, wide), F32)] * 2 + [flat, square],
        (*all_stats, high, *pieces, w2, x2), 12, flops=unit)
    back2 = send(dq2, shift_y(-2))
    dq0, dq1, dq3, dkr, dvr, o0, o1, o2, o3 = call(
        local_kernel, "local", [flat] * 3 + [small, small] + [both] * 4,
        (factors, delta, *pieces, kr, w0, w1, w2, w3, x0, x1, x3, xr, ds2,
         m0, m1, m2, m3, q0, q1, q2, q3), 16, flops=11 * unit)
    dq1, unused = lax.optimization_barrier((dq1, back2))
    total = combine(o0, [send(x, shift_z(-d)) for d, x in ((1, o1), (3, o3), (2, o2))])
    returned = [send(x, shift_y(-d)) for d, x in ((1, dq1), (3, dq3))] + [back2]
    grad_queries = combine(dq0, returned)
    return grad_queries, total[:part], total[part:], dkr, dvr


def solution(mesh):
    spec = P(("group", "resp"), "tp")
    return jax.shard_map(
        body,
        mesh=mesh,
        in_specs=(spec,) * 6 + (P(("group", "resp")),),
        out_specs=(spec,) * 5,
        check_vma=False,
    )
```

```python
import functools

import jax
import jax.numpy as jnp
from jax import lax
from jax.experimental import pallas as pl
from jax.experimental.pallas import tpu as pltpu
from jax.sharding import PartitionSpec as P

HEAD_DIM = 128
SIDE = 4
LOG2E = 1.4426950408889634
BF16 = jnp.bfloat16
F32 = jnp.float32


def dot(a, b, ca, cb):
    return lax.dot_general(a, b, (((ca,), (cb,)), ((), ())), preferred_element_type=F32)


def stack_heads(q_ref):
    heads = q_ref.shape[1] // HEAD_DIM
    return jnp.concatenate([q_ref[:, h * HEAD_DIM : (h + 1) * HEAD_DIM] for h in range(heads)], 0)


def prepare_kernel(len_hbm, q_hbm, g_hbm, k_hbm, v_hbm, kr_hbm, vr_hbm,
                   mt_ref, q_ref, kv_ref, kr_ref, vr_ref, g_ref, len_ref, sems):
    piece = k_hbm.shape[0]
    pairs = (
        (len_hbm, len_ref),
        (g_hbm, g_ref),
        (k_hbm, kv_ref.at[pl.ds(0, piece)]),
        (v_hbm, kv_ref.at[pl.ds(piece, piece)]),
        (q_hbm, q_ref),
        (kr_hbm, kr_ref),
        (vr_hbm, vr_ref),
    )
    copies = [pltpu.make_async_copy(a, b, sems.at[n]) for n, (a, b) in enumerate(pairs)]
    for copy in copies:
        copy.start()
    copies[0].wait()
    copies[1].wait()
    rows, cols = g_ref.shape
    alive = lax.broadcasted_iota(jnp.int32, (rows, cols), 0) < len_ref[0]
    masked = jnp.where(alive, g_ref[...].astype(F32), 0.0)
    for h in range(cols // HEAD_DIM):
        part = masked[:, h * HEAD_DIM : (h + 1) * HEAD_DIM]
        mt_ref[:, h * rows : (h + 1) * rows] = part.T.astype(BF16)
    for copy in copies[2:]:
        copy.wait()


def plane_of(pieces, part):
    size = pieces[0].shape[0] // 2
    return jnp.concatenate([p[part * size : (part + 1) * size, :] for p in pieces], 0)


def summary(highest, totals, n, high_ref, lse_ref):
    high = highest * (HEAD_DIM**-0.5 * LOG2E)
    high_ref[n : n + 1, :] = high
    lse_ref[n : n + 1, :] = high + jnp.log2(totals)


def respond(jobs, values, high_ref, lse_ref):
    group, step, small = 16, 256, 64
    scale = HEAD_DIM**-0.5 * LOG2E
    before = None
    for n in range(len(jobs) + 1):
        scoring, weighing = [], []
        if n < len(jobs):
            q_ref, parts, w_ref, a_ref, s_ref = jobs[n]
            q = stack_heads(q_ref)
            wide = q.shape[0]
            top = jnp.full((group, wide), -jnp.inf, F32)
            base = 0
            for keys, mask in parts:
                for r in range(0, keys.shape[0], step):
                    block = keys[r : r + step, :]
                    scoring.append((block, mask, base))
                    base += block.shape[0]
        if n:
            weighing = list(range(0, jobs[n - 1][4].shape[0], small))
            totals = jnp.zeros((group, wide), F32)
        turns = max(len(scoring), 1)
        share = -(-len(weighing) // turns)
        for turn in range(turns):
            if scoring:
                block, mask, base = scoring[turn]
                size = block.shape[0]
                x = dot(block, q, 1, 1)
                if mask is not None:
                    x = jnp.where(mask, x, -jnp.inf)
                jobs[n][4][base : base + size, :] = x
                top = jnp.maximum(top, jnp.max(x.reshape(size // group, group, wide), 0))
            for t in weighing[turn * share : (turn + 1) * share]:
                w = jnp.exp2((jobs[n - 1][4][t : t + small, :] - before) * scale)
                jobs[n - 1][2][t : t + small, :] = w.astype(BF16)
                totals = totals + jnp.sum(w.reshape(small // group, group, wide), 0)
        if n:
            summary(before, jnp.sum(totals, 0, keepdims=True), n - 1, high_ref, lse_ref)
            jobs[n - 1][3][...] = dot(values[n - 1], jobs[n - 1][2][...], 0, 0)
        if n < len(jobs):
            before = jnp.max(top, 0, keepdims=True)


def first_kernel(q0, q1, kr, vr, p0, p1, w0, w1, high_ref, lse_ref, a0, a1, s0, s1):
    rows, wide = kr.shape[0], w1.shape[1]
    keys, values = plane_of((p0, p1), 0), plane_of((p0, p1), 1)
    key_pos = lax.broadcasted_iota(jnp.int32, (rows, wide), 0)
    token = lax.broadcasted_iota(jnp.int32, (rows, wide), 1) % rows
    jobs = (
        (q0, [(kr[...], key_pos <= token), (keys, None)], w0, a0, s0),
        (q1, [(keys, None)], w1, a1, s1),
    )
    respond(jobs, (jnp.concatenate([vr[...], values], 0), values), high_ref, lse_ref)


def second_kernel(q0, q1, q2, q3, p0, p1, p3, p2, w0, w1, w2, w3, high_ref, lse_ref, a0, a1, a2, a3,
                  s0, s1, s2, s3):
    keys, values = plane_of((p3, p2), 0), plane_of((p3, p2), 1)
    pieces = (p0, p1, p3, p2)
    every, all_values = plane_of(pieces, 0), plane_of(pieces, 1)
    jobs = (
        (q0, [(keys, None)], w0, a0, s0),
        (q1, [(keys, None)], w1, a1, s1),
        (q2, [(every, None)], w2, a2, s2),
        (q3, [(every, None)], w3, a3, s3),
    )
    respond(jobs, (values, values, all_values, all_values), high_ref, lse_ref)


def delta_kernel(high01, highs, lse01, lses, a0, a1, b0, b1, b2, b3, m0, m1, m2, m3,
                 high_ref, stat_ref):
    for d, m in enumerate((m0, m1, m2, m3)):
        high_b, lse = highs[d : d + 1, :], lses[d : d + 1, :]
        high_a = high_b
        total = (b0, b1, b2, b3)[d][...]
        if d < 2:
            a = (a0, a1)[d]
            high_a = high01[d : d + 1, :]
            lse_a = lse01[d : d + 1, :]
            top = jnp.maximum(lse, lse_a)
            lse = top + jnp.log2(jnp.exp2(lse - top) + jnp.exp2(lse_a - top))
            total = total * jnp.exp2(high_b - lse) + a[...] * jnp.exp2(high_a - lse)
        else:
            total = total * jnp.exp2(high_b - lse)
        high_ref[2 * d : 2 * d + 1, :] = high_a
        high_ref[2 * d + 1 : 2 * d + 2, :] = high_b
        stat_ref[2 * d : 2 * d + 1, :] = lse
        stat_ref[2 * d + 1 : 2 * d + 2, :] = jnp.sum(m[...].astype(F32) * total, 0, keepdims=True)


def product_kernel(stat_ref, p0, p1, p3, p2, vr, m0, m1, m2, m3, x0, x1, x2, x3, xr):
    values = plane_of((p0, p1, p3, p2), 1)
    for m, x in ((m1, x1), (m3, x3), (m2, x2), (m0, x0)):
        x[...] = dot(values, m[...], 1, 0)
    xr[...] = dot(vr[...], m0[...], 1, 0)


def settle(stats, high_ref, d):
    parts = []
    for e, ref in enumerate(stats):
        row = 2 * ((d - e) % SIDE)
        parts.append((ref[row : row + 1, :], ref[row + 1 : row + 2, :]))
    highest = parts[0][0]
    for lse, term in parts[1:]:
        highest = jnp.maximum(highest, lse)
    totals = jnp.zeros_like(highest)
    delta = jnp.zeros_like(highest)
    for lse, term in parts:
        share = jnp.exp2(lse - highest)
        totals = totals + share
        delta = delta + term * share
    inverse = 1.0 / totals
    factors = jnp.exp2(high_ref[2 * d : 2 * d + 2, :] - highest) * inverse
    return factors, delta * inverse


def turn_back(total, out):
    rows = out.shape[0]
    total = total * HEAD_DIM**-0.5
    for h in range(total.shape[1] // rows):
        part = total[:, h * rows : (h + 1) * rows]
        out[:, h * HEAD_DIM : (h + 1) * HEAD_DIM] = part.T.astype(BF16)


def remote_kernel(t0, t1, t2, t3, high_ref, p0, p1, p3, p2, w2, x2,
                  factor_ref, delta_ref, q2, ds2):
    stats = (t0, t1, t2, t3)
    for d in range(SIDE):
        factors, delta = settle(stats, high_ref, d)
        factor_ref[2 * d : 2 * d + 2, :] = factors
        delta_ref[d : d + 1, :] = delta
        if d == 2:
            ds = w2[...] * ((x2[...] - delta) * factors[0:1, :]).astype(BF16)
            ds2[...] = ds
            turn_back(dot(plane_of((p0, p1, p3, p2), 0), ds, 0, 0), q2)


def local_kernel(factor_ref, delta_ref, p0, p1, p3, p2, kr, w0a, w0b, w1a, w1b, w2, w3,
                 x0, x1, x3, xr, ds2, m0, m1, m2, m3, q0, q1, q2, q3,
                 dq0, dq1, dq3, dkr_ref, dvr_ref, o0, o1, o3, o2):
    rows = kr.shape[0]
    size = p0.shape[0] // 2
    half = w1a.shape[0]
    scale = HEAD_DIM**-0.5
    plane_keys = plane_of((p0, p1, p3, p2), 0)

    def masked(m, d, n):
        return (m[...].astype(F32) * factor_ref[2 * d + n : 2 * d + n + 1, :]).astype(BF16)

    q, g = stack_heads(q2), masked(m2, 2, 0)
    keys = [dot(ds2[n * half : (n + 1) * half, :], q, 1, 0) for n in range(2)]
    values = [dot(w2[n * half : (n + 1) * half, :], g, 1, 1) for n in range(2)]
    for d, q_ref, m, ws, x, out in (
        (1, q1, m1, (w1a, w1b), x1, dq1),
        (3, q3, m3, (w3, w3), x3, dq3),
        (0, q0, m0, (w0a, w0b), x0, dq0),
    ):
        delta = delta_ref[d : d + 1, :]
        q = stack_heads(q_ref)
        grad = None
        for n, w in enumerate(ws):
            factor = factor_ref[2 * d + n : 2 * d + n + 1, :]
            g = masked(m, d, n)
            skip = 0
            if w is w0a:
                skip = rows
                near = w[0:rows, :]
                ds = near * ((xr[...] - delta) * factor).astype(BF16)
                dvr_ref[...] = dot(near, g, 1, 1).astype(BF16)
                dkr_ref[...] = (dot(ds, q, 1, 0) * scale).astype(BF16)
                grad = dot(kr[...], ds, 0, 0)
            here = slice(n * half, (n + 1) * half)
            weights = w[here, :] if w is w3 else w[skip : skip + half, :]
            ds = weights * ((x[here, :] - delta) * factor).astype(BF16)
            values[n] = values[n] + dot(weights, g, 1, 1)
            keys[n] = keys[n] + dot(ds, q, 1, 0)
            part = dot(plane_keys[here, :], ds, 0, 0)
            grad = part if grad is None else grad + part
        turn_back(grad, out)
    for n, outs in enumerate(((o0, o1), (o3, o2))):
        k = (keys[n] * scale).astype(BF16)
        v = values[n].astype(BF16)
        for i, out in enumerate(outs):
            out[0:size, :] = k[i * size : (i + 1) * size, :]
            out[size : 2 * size, :] = v[i * size : (i + 1) * size, :]


def shift_y(d):
    return [(y * SIDE + z, (y + d) % SIDE * SIDE + z) for y in range(SIDE) for z in range(SIDE)]


def shift_z(d):
    return [(y * SIDE + z, y * SIDE + (z + d) % SIDE) for y in range(SIDE) for z in range(SIDE)]


def send(x, perm):
    return lax.ppermute(x, "resp", perm)


def combine(own, received):
    own = own.astype(F32)
    for x in received:
        own = own + x.astype(F32)
    return own.astype(BF16)


def from_others(x, shift):
    one, three, two = (send(x, shift(d)) for d in (1, 3, 2))
    return one, two, three


def call(kernel, name, outs, inputs, memory, scratch=(), flops=0, exps=0, space=pltpu.VMEM):
    return pl.pallas_call(
        kernel,
        out_shape=[jax.ShapeDtypeStruct(*o) for o in outs],
        in_specs=[pl.BlockSpec(memory_space=space)] * len(inputs),
        out_specs=[pl.BlockSpec(memory_space=pltpu.VMEM)] * len(outs),
        scratch_shapes=list(scratch),
        compiler_params=pltpu.CompilerParams(vmem_limit_bytes=memory * 2**20),
        cost_estimate=pl.CostEstimate(flops=flops, bytes_accessed=2**20, transcendentals=exps),
        name=name,
    )(*inputs)


def body(queries, prompt_keys, prompt_values, resp_keys, resp_values, grad_out, lengths):
    rows, cols = queries.shape
    part = prompt_keys.shape[0]
    plane = SIDE * part
    wide = rows * cols // HEAD_DIM
    unit = 2 * wide * plane * HEAD_DIM
    turned = ((HEAD_DIM, wide), BF16)
    turned_wide = ((HEAD_DIM, wide), F32)
    small = ((rows, HEAD_DIM), BF16)
    flat = ((rows, cols), BF16)
    both = ((2 * part, HEAD_DIM), BF16)
    square = ((plane, wide), BF16)
    square_wide = ((plane, wide), F32)

    q1, q3 = (send(queries, shift_y(d)) for d in (1, 3))
    params = (queries, grad_out, prompt_keys, prompt_values, resp_keys, resp_values)
    m0, q0, piece, kr, vr = call(
        prepare_kernel, "prepare", [turned, flat, both, small, small],
        [lengths] + [pltpu.with_memory_space_constraint(x, pltpu.HBM) for x in params], 8,
        [pltpu.VMEM((rows, cols), BF16), pltpu.SMEM((1,), jnp.int32),
         pltpu.SemaphoreType.DMA((7,))], space=pltpu.HBM)
    p1, p3 = (send(piece, shift_z(d)) for d in (1, 3))
    pieces = (piece, p1, p3, send(p3, shift_z(3)))
    later, unused = lax.optimization_barrier((q1, p1))
    q2 = send(later, shift_y(1))
    m1, m3 = (send(m0, shift_y(d)) for d in (1, 3))
    m2 = send(m3, shift_y(3))
    half = plane // 2
    tall, short = ((half + rows, wide), BF16), ((half, wide), BF16)
    line = ((2, wide), F32)
    w0a, w1a, high01, lse01, a0, a1 = call(
        first_kernel, "first", [tall, short, line, line] + [turned_wide] * 2,
        (q0, q1, kr, vr, piece, p1), 16,
        [pltpu.VMEM(x[0], F32) for x in (tall, short)], flops=3 * unit, exps=plane * wide)
    w0b, w1b, w2, w3, highs, lses, b0, b1, b2, b3 = call(
        second_kernel, "second",
        [short, short, square, square] + [((SIDE, wide), F32)] * 2 + [turned_wide] * 4,
        (q0, q1, q2, q3, *pieces), 24,
        [pltpu.VMEM(x[0], F32) for x in (short, short, square, square)], flops=6 * unit,
        exps=3 * plane * wide)
    high, stat = call(
        delta_kernel, "delta", [((2 * SIDE, wide), F32)] * 2,
        (high01, highs, lse01, lses, a0, a1, b0, b1, b2, b3, m0, m1, m2, m3), 8,
        flops=unit // 2)
    all_stats = (stat, *from_others(stat, shift_y))
    x0, x1, x2, x3, xr = call(
        product_kernel, "product", [square_wide] * 4 + [((rows, wide), F32)],
        (stat, *pieces, vr, m0, m1, m2, m3), 12, flops=4 * unit)
    factors, delta, dq2, ds2 = call(
        remote_kernel, "remote",
        [((2 * SIDE, wide), F32), ((SIDE, wide), F32), flat, square],
        (*all_stats, high, *pieces, w2, x2), 12, flops=unit)
    back2 = send(dq2, shift_y(-2))
    dq0, dq1, dq3, dkr, dvr, o0, o1, o3, o2 = call(
        local_kernel, "local", [flat] * 3 + [small, small] + [both] * 4,
        (factors, delta, *pieces, kr, w0a, w0b, w1a, w1b, w2, w3, x0, x1, x3, xr, ds2,
         m0, m1, m2, m3, q0, q1, q2, q3), 16, flops=11 * unit)
    dq1, unused = lax.optimization_barrier((dq1, back2))
    total = combine(o0, [send(x, shift_z(-d)) for d, x in ((2, o2), (1, o1), (3, o3))])
    returned = [send(x, shift_y(-d)) for d, x in ((1, dq1), (3, dq3))] + [back2]
    grad_queries = combine(dq0, returned)
    return grad_queries, total[:part], total[part:], dkr, dvr


def solution(mesh):
    spec = P(("group", "resp"), "tp")
    return jax.shard_map(
        body,
        mesh=mesh,
        in_specs=(spec,) * 6 + (P(("group", "resp")),),
        out_specs=(spec,) * 5,
        check_vma=False,
    )
```

```python
import functools

import jax
import jax.numpy as jnp
from jax import lax
from jax.experimental import pallas as pl
from jax.experimental.pallas import tpu as pltpu
from jax.sharding import PartitionSpec as P

HEAD_DIM = 128
SIDE = 4
LOG2E = 1.4426950408889634
BF16 = jnp.bfloat16
F32 = jnp.float32


def dot(a, b, ca, cb):
    return lax.dot_general(a, b, (((ca,), (cb,)), ((), ())), preferred_element_type=F32)


def stack_heads(q_ref):
    heads = q_ref.shape[1] // HEAD_DIM
    return jnp.concatenate([q_ref[:, h * HEAD_DIM : (h + 1) * HEAD_DIM] for h in range(heads)], 0)


def prepare_kernel(len_hbm, q_hbm, g_hbm, k_hbm, v_hbm, kr_hbm, vr_hbm,
                   mt_ref, q_ref, kv_ref, kr_ref, vr_ref, g_ref, len_ref, sems):
    piece = k_hbm.shape[0]
    pairs = (
        (len_hbm, len_ref),
        (g_hbm, g_ref),
        (k_hbm, kv_ref.at[pl.ds(0, piece)]),
        (v_hbm, kv_ref.at[pl.ds(piece, piece)]),
        (q_hbm, q_ref),
        (kr_hbm, kr_ref),
        (vr_hbm, vr_ref),
    )
    copies = [pltpu.make_async_copy(a, b, sems.at[n]) for n, (a, b) in enumerate(pairs)]
    for copy in copies:
        copy.start()
    copies[0].wait()
    copies[1].wait()
    rows, cols = g_ref.shape
    alive = lax.broadcasted_iota(jnp.int32, (rows, cols), 0) < len_ref[0]
    masked = jnp.where(alive, g_ref[...].astype(F32), 0.0)
    for h in range(cols // HEAD_DIM):
        part = masked[:, h * HEAD_DIM : (h + 1) * HEAD_DIM]
        mt_ref[:, h * rows : (h + 1) * rows] = part.T.astype(BF16)
    for copy in copies[2:]:
        copy.wait()


def plane_of(pieces, part):
    size = pieces[0].shape[0] // 2
    return jnp.concatenate([p[part * size : (part + 1) * size, :] for p in pieces], 0)


def summary(highest, totals, n, high_ref, lse_ref):
    high = highest * (HEAD_DIM**-0.5 * LOG2E)
    high_ref[n : n + 1, :] = high
    lse_ref[n : n + 1, :] = high + jnp.log2(totals)


def respond(jobs, values, high_ref, lse_ref):
    group, step, small = 16, 256, 64
    scale = HEAD_DIM**-0.5 * LOG2E
    before = None
    for n in range(len(jobs) + 1):
        scoring, weighing = [], []
        if n < len(jobs):
            q_ref, parts, w_ref, a_ref, s_ref = jobs[n]
            q = stack_heads(q_ref)
            wide = q.shape[0]
            top = jnp.full((group, wide), -jnp.inf, F32)
            base = 0
            for keys, mask in parts:
                for r in range(0, keys.shape[0], step):
                    block = keys[r : r + step, :]
                    scoring.append((block, mask, base))
                    base += block.shape[0]
        if n:
            weighing = list(range(0, jobs[n - 1][4].shape[0], small))
            totals = jnp.zeros((group, wide), F32)
        turns = max(len(scoring), 1)
        share = -(-len(weighing) // turns)
        for turn in range(turns):
            if scoring:
                block, mask, base = scoring[turn]
                size = block.shape[0]
                x = dot(block, q, 1, 1)
                if mask is not None:
                    x = jnp.where(mask, x, -jnp.inf)
                jobs[n][4][base : base + size, :] = x
                top = jnp.maximum(top, jnp.max(x.reshape(size // group, group, wide), 0))
            for t in weighing[turn * share : (turn + 1) * share]:
                w = jnp.exp2((jobs[n - 1][4][t : t + small, :] - before) * scale)
                jobs[n - 1][2][t : t + small, :] = w.astype(BF16)
                totals = totals + jnp.sum(w.reshape(small // group, group, wide), 0)
        if n:
            summary(before, jnp.sum(totals, 0, keepdims=True), n - 1, high_ref, lse_ref)
            jobs[n - 1][3][...] = dot(values[n - 1], jobs[n - 1][2][...], 0, 0)
        if n < len(jobs):
            before = jnp.max(top, 0, keepdims=True)


def first_kernel(q0, q1, kr, vr, p0, p1, w0, w1, high_ref, lse_ref, a0, a1, s0, s1):
    rows, wide = kr.shape[0], w1.shape[1]
    keys, values = plane_of((p0, p1), 0), plane_of((p0, p1), 1)
    key_pos = lax.broadcasted_iota(jnp.int32, (rows, wide), 0)
    token = lax.broadcasted_iota(jnp.int32, (rows, wide), 1) % rows
    jobs = (
        (q0, [(kr[...], key_pos <= token), (keys, None)], w0, a0, s0),
        (q1, [(keys, None)], w1, a1, s1),
    )
    respond(jobs, (jnp.concatenate([vr[...], values], 0), values), high_ref, lse_ref)


def second_kernel(q0, q1, q2, q3, p0, p1, p3, p2, w0, w1, w2, w3, high_ref, lse_ref, a0, a1, a2, a3,
                  s0, s1, s2, s3):
    keys, values = plane_of((p3, p2), 0), plane_of((p3, p2), 1)
    pieces = (p0, p1, p3, p2)
    every, all_values = plane_of(pieces, 0), plane_of(pieces, 1)
    jobs = (
        (q0, [(keys, None)], w0, a0, s0),
        (q1, [(keys, None)], w1, a1, s1),
        (q2, [(every, None)], w2, a2, s2),
        (q3, [(every, None)], w3, a3, s3),
    )
    respond(jobs, (values, values, all_values, all_values), high_ref, lse_ref)


def delta_kernel(high01, highs, lse01, lses, a0, a1, b0, b1, b2, b3, m0, m1, m2, m3,
                 high_ref, stat_ref):
    for d, m in enumerate((m0, m1, m2, m3)):
        high_b, lse = highs[d : d + 1, :], lses[d : d + 1, :]
        high_a = high_b
        total = (b0, b1, b2, b3)[d][...]
        if d < 2:
            a = (a0, a1)[d]
            high_a = high01[d : d + 1, :]
            lse_a = lse01[d : d + 1, :]
            top = jnp.maximum(lse, lse_a)
            lse = top + jnp.log2(jnp.exp2(lse - top) + jnp.exp2(lse_a - top))
            total = total * jnp.exp2(high_b - lse) + a[...] * jnp.exp2(high_a - lse)
        else:
            total = total * jnp.exp2(high_b - lse)
        high_ref[2 * d : 2 * d + 1, :] = high_a
        high_ref[2 * d + 1 : 2 * d + 2, :] = high_b
        stat_ref[2 * d : 2 * d + 1, :] = lse
        stat_ref[2 * d + 1 : 2 * d + 2, :] = jnp.sum(m[...].astype(F32) * total, 0, keepdims=True)


def product_kernel(stat_ref, p0, p1, p3, p2, vr, m0, m1, m2, m3, x0, x1, x2, x3, xr):
    values = plane_of((p0, p1, p3, p2), 1)
    for m, x in ((m1, x1), (m3, x3), (m2, x2), (m0, x0)):
        x[...] = dot(values, m[...], 1, 0)
    xr[...] = dot(vr[...], m0[...], 1, 0)


def settle(stats, high_ref, d):
    parts = []
    for e, ref in enumerate(stats):
        row = 2 * ((d - e) % SIDE)
        parts.append((ref[row : row + 1, :], ref[row + 1 : row + 2, :]))
    highest = parts[0][0]
    for lse, term in parts[1:]:
        highest = jnp.maximum(highest, lse)
    totals = jnp.zeros_like(highest)
    delta = jnp.zeros_like(highest)
    for lse, term in parts:
        share = jnp.exp2(lse - highest)
        totals = totals + share
        delta = delta + term * share
    inverse = 1.0 / totals
    factors = jnp.exp2(high_ref[2 * d : 2 * d + 2, :] - highest) * inverse
    return factors, delta * inverse


def turn_back(total, out):
    rows = out.shape[0]
    total = total * HEAD_DIM**-0.5
    for h in range(total.shape[1] // rows):
        part = total[:, h * rows : (h + 1) * rows]
        out[:, h * HEAD_DIM : (h + 1) * HEAD_DIM] = part.T.astype(BF16)


def local_kernel(t0, t1, t2, t3, high_ref, p0, p1, p3, p2, kr, w0a, w0b, w1a, w1b, w2, w3,
                 x0, x1, x2, x3, xr, m0, m1, m2, m3, q0, q1, q2, q3,
                 dq0, dq1, dq2, dq3, dkr_ref, dvr_ref, o0, o1, o3, o2, factor_ref, delta_ref):
    for d in range(SIDE):
        factors, delta = settle((t0, t1, t2, t3), high_ref, d)
        factor_ref[2 * d : 2 * d + 2, :] = factors
        delta_ref[d : d + 1, :] = delta
    rows = kr.shape[0]
    size = p0.shape[0] // 2
    half = w1a.shape[0]
    scale = HEAD_DIM**-0.5
    plane_keys = plane_of((p0, p1, p3, p2), 0)

    def masked(m, d, n):
        return (m[...].astype(F32) * factor_ref[2 * d + n : 2 * d + n + 1, :]).astype(BF16)

    keys, values = [None, None], [None, None]

    def plus(total, part):
        return part if total is None else total + part

    for d, q_ref, m, ws, x, out in (
        (2, q2, m2, (w2, w2), x2, dq2),
        (1, q1, m1, (w1a, w1b), x1, dq1),
        (3, q3, m3, (w3, w3), x3, dq3),
        (0, q0, m0, (w0a, w0b), x0, dq0),
    ):
        delta = delta_ref[d : d + 1, :]
        q = stack_heads(q_ref)
        grad = None
        for n, w in enumerate(ws):
            factor = factor_ref[2 * d + n : 2 * d + n + 1, :]
            g = masked(m, d, n)
            skip = 0
            if w is w0a:
                skip = rows
                near = w[0:rows, :]
                ds = near * ((xr[...] - delta) * factor).astype(BF16)
                dvr_ref[...] = dot(near, g, 1, 1).astype(BF16)
                dkr_ref[...] = (dot(ds, q, 1, 0) * scale).astype(BF16)
                grad = dot(kr[...], ds, 0, 0)
            here = slice(n * half, (n + 1) * half)
            weights = w[here, :] if w is w3 or w is w2 else w[skip : skip + half, :]
            ds = weights * ((x[here, :] - delta) * factor).astype(BF16)
            values[n] = plus(values[n], dot(weights, g, 1, 1))
            keys[n] = plus(keys[n], dot(ds, q, 1, 0))
            part = dot(plane_keys[here, :], ds, 0, 0)
            grad = part if grad is None else grad + part
        turn_back(grad, out)
    for n, outs in enumerate(((o0, o1), (o3, o2))):
        k = (keys[n] * scale).astype(BF16)
        v = values[n].astype(BF16)
        for i, out in enumerate(outs):
            out[0:size, :] = k[i * size : (i + 1) * size, :]
            out[size : 2 * size, :] = v[i * size : (i + 1) * size, :]


def shift_y(d):
    return [(y * SIDE + z, (y + d) % SIDE * SIDE + z) for y in range(SIDE) for z in range(SIDE)]


def shift_z(d):
    return [(y * SIDE + z, y * SIDE + (z + d) % SIDE) for y in range(SIDE) for z in range(SIDE)]


def send(x, perm):
    return lax.ppermute(x, "resp", perm)


def combine(own, received):
    own = own.astype(F32)
    for x in received:
        own = own + x.astype(F32)
    return own.astype(BF16)


def from_others(x, shift):
    one, three, two = (send(x, shift(d)) for d in (1, 3, 2))
    return one, two, three


def call(kernel, name, outs, inputs, memory, scratch=(), flops=0, exps=0, space=pltpu.VMEM):
    return pl.pallas_call(
        kernel,
        out_shape=[jax.ShapeDtypeStruct(*o) for o in outs],
        in_specs=[pl.BlockSpec(memory_space=space)] * len(inputs),
        out_specs=[pl.BlockSpec(memory_space=pltpu.VMEM)] * len(outs),
        scratch_shapes=list(scratch),
        compiler_params=pltpu.CompilerParams(vmem_limit_bytes=memory * 2**20),
        cost_estimate=pl.CostEstimate(flops=flops, bytes_accessed=2**20, transcendentals=exps),
        name=name,
    )(*inputs)


def body(queries, prompt_keys, prompt_values, resp_keys, resp_values, grad_out, lengths):
    rows, cols = queries.shape
    part = prompt_keys.shape[0]
    plane = SIDE * part
    wide = rows * cols // HEAD_DIM
    unit = 2 * wide * plane * HEAD_DIM
    turned = ((HEAD_DIM, wide), BF16)
    turned_wide = ((HEAD_DIM, wide), F32)
    small = ((rows, HEAD_DIM), BF16)
    flat = ((rows, cols), BF16)
    both = ((2 * part, HEAD_DIM), BF16)
    square = ((plane, wide), BF16)
    square_wide = ((plane, wide), F32)

    q1, q3 = (send(queries, shift_y(d)) for d in (1, 3))
    params = (queries, grad_out, prompt_keys, prompt_values, resp_keys, resp_values)
    m0, q0, piece, kr, vr = call(
        prepare_kernel, "prepare", [turned, flat, both, small, small],
        [lengths] + [pltpu.with_memory_space_constraint(x, pltpu.HBM) for x in params], 8,
        [pltpu.VMEM((rows, cols), BF16), pltpu.SMEM((1,), jnp.int32),
         pltpu.SemaphoreType.DMA((7,))], space=pltpu.HBM)
    p1, p3 = (send(piece, shift_z(d)) for d in (1, 3))
    pieces = (piece, p1, p3, send(p3, shift_z(3)))
    later, unused = lax.optimization_barrier((q1, p1))
    q2 = send(later, shift_y(1))
    m1, m3 = (send(m0, shift_y(d)) for d in (1, 3))
    m2 = send(m3, shift_y(3))
    half = plane // 2
    tall, short = ((half + rows, wide), BF16), ((half, wide), BF16)
    line = ((2, wide), F32)
    w0a, w1a, high01, lse01, a0, a1 = call(
        first_kernel, "first", [tall, short, line, line] + [turned_wide] * 2,
        (q0, q1, kr, vr, piece, p1), 16,
        [pltpu.VMEM(x[0], F32) for x in (tall, short)], flops=3 * unit, exps=plane * wide)
    w0b, w1b, w2, w3, highs, lses, b0, b1, b2, b3 = call(
        second_kernel, "second",
        [short, short, square, square] + [((SIDE, wide), F32)] * 2 + [turned_wide] * 4,
        (q0, q1, q2, q3, *pieces), 24,
        [pltpu.VMEM(x[0], F32) for x in (short, short, square, square)], flops=6 * unit,
        exps=3 * plane * wide)
    high, stat = call(
        delta_kernel, "delta", [((2 * SIDE, wide), F32)] * 2,
        (high01, highs, lse01, lses, a0, a1, b0, b1, b2, b3, m0, m1, m2, m3), 8,
        flops=unit // 2)
    all_stats = (stat, *from_others(stat, shift_y))
    x0, x1, x2, x3, xr = call(
        product_kernel, "product", [square_wide] * 4 + [((rows, wide), F32)],
        (stat, *pieces, vr, m0, m1, m2, m3), 12, flops=4 * unit)
    dq0, dq1, dq2, dq3, dkr, dvr, o0, o1, o3, o2 = call(
        local_kernel, "local", [flat] * 4 + [small, small] + [both] * 4,
        (*all_stats, high, *pieces, kr, w0a, w0b, w1a, w1b, w2, w3, x0, x1, x2, x3, xr,
         m0, m1, m2, m3, q0, q1, q2, q3), 16,
        [pltpu.VMEM((2 * SIDE, wide), F32), pltpu.VMEM((SIDE, wide), F32)], flops=12 * unit)
    returned = [send(x, shift_y(-d)) for d, x in ((2, dq2), (1, dq1), (3, dq3))]
    o3, unused = lax.optimization_barrier((o3, returned[0]))
    total = combine(o0, [send(x, shift_z(-d)) for d, x in ((2, o2), (1, o1), (3, o3))])
    grad_queries = combine(dq0, returned)
    return grad_queries, total[:part], total[part:], dkr, dvr


def solution(mesh):
    spec = P(("group", "resp"), "tp")
    return jax.shard_map(
        body,
        mesh=mesh,
        in_specs=(spec,) * 6 + (P(("group", "resp")),),
        out_specs=(spec,) * 5,
        check_vma=False,
    )
```
